32 devices in a mesh: llm: 4 (over y, x), enc: 8 (over z, core).
Axes of the slice: x: 2, y: 2, z: 4, core: 2. Of those that a mesh axis runs over, the one named last changes fastest.
Arguments:
- token_gradient: bfloat16 [64, 128, 8192], P('enc', None, 'llm'), may hold values from -6 to 6
- projection: bfloat16 [1280, 8192], P(None, 'llm'), may hold values from -0.0625 to 0.0625
- clip_length: int32 [128], P('enc'), may hold values from 16 to 32, as said below
- clip_offset: int32 [128], P('enc'), may hold values from 0 to 96, as said below
- clip_home: int32 [128], P('enc'), may hold values from 0 to 127, as said below
- block_input: bfloat16 [128, 32, 1280], P('enc'), may hold values from -6 to 6
- block_output: bfloat16 [128, 32, 1280], P('enc'), may hold values from -6 to 6
- norm_gain: float32 [1280], replicated, may hold values from 0.1 to 1.9
- norm_bias: float32 [1280], replicated, may hold values from -3 to 3
- up_weight: bfloat16 [1280, 5120], P('enc', 'llm'), may hold values from -0.15625 to 0.15625
- up_bias: float32 [5120], P('llm'), may hold values from -3 to 3
- down_weight: bfloat16 [5120, 1280], P('llm', 'enc'), may hold values from -0.078125 to 0.078125
- post_gain: float32 [1280], replicated, may hold values from 0.1 to 1.9
Outputs:
- input_gradient: bfloat16 [128, 32, 1280], P('enc', None, 'llm')
- up_gradient: float32 [1280, 5120], P('enc', 'llm')
- down_gradient: float32 [5120, 1280], P('llm', 'enc')
The draws below stay inside these ranges and needn't reach their ends.
Inputs may be any that keep to these rules, and one draw needn't show every extreme that they name: `clip_length`: each entry of an aligned block of 16 entries is at most 32, and every block holds one entry equal to 32. Clip k starts in part k % 2 of its sequence, the parts being 64 rows long, and clip_offset + 32 stays within that part. `clip_home`: A permutation of the 128 encoder slots; slot j belongs to encoder index j // 16; the clips of one aligned block of 16 entries go to one encoder index at most 2 times, and some encoder index receives exactly 2 of them.
All inputs are finite; a program needn't handle non-finite values.
Results may differ from the reference program's by a relative error of at most 0.0068.
Values may be sent and summed in bfloat16 or wider, within the bound.
A program may use at most 128 MiB of HBM per device.

```python
import jax
import jax.numpy as jnp
from jax import lax

D = 1280
FF = 5120
HL = 8192
CLIPS_DEV = 16
FRAMES = 32
CPS = 2
SEQ_LEN = 128
CLIPS = 128
SEQS = 64
N_ENC = 8


def draw_clip_home(key, part):
    base_key = jax.random.fold_in(key, 101)
    sender_order = jax.random.permutation(jax.random.fold_in(base_key, 1), N_ENC)
    target_order = jax.random.permutation(jax.random.fold_in(base_key, 2), N_ENC)
    slot_key = jax.random.fold_in(base_key, 3)
    clip_index = jnp.arange(CLIPS, dtype=jnp.int32)
    sender = clip_index // CLIPS_DEV
    within = clip_index % CLIPS_DEV
    target = target_order[(sender_order[sender] + within) % N_ENC]

    def slot_order(receiver):
        return jax.random.permutation(jax.random.fold_in(slot_key, receiver), CLIPS_DEV)
    slot_tables = jax.vmap(slot_order)(jnp.arange(N_ENC, dtype=jnp.int32))
    chosen_slot = slot_tables[target, within]
    return (target * CLIPS_DEV + chosen_slot).astype(jnp.int32)


def draw_clip_length(key, part):
    base_key = jax.random.fold_in(key, 202)
    lengths = jax.random.randint(jax.random.fold_in(base_key, 1), (CLIPS,), FRAMES // 2, FRAMES + 1)
    longest = jax.random.randint(jax.random.fold_in(base_key, 2), (N_ENC,), 0, CLIPS_DEV)
    clip_index = jnp.arange(CLIPS, dtype=jnp.int32)
    full_clip = clip_index % CLIPS_DEV == longest[clip_index // CLIPS_DEV]
    return jnp.where(full_clip, FRAMES, lengths).astype(jnp.int32)


def draw_clip_offset(key, part):
    base_key = jax.random.fold_in(key, 303)
    segment = SEQ_LEN // CPS
    clip_index = jnp.arange(CLIPS, dtype=jnp.int32)
    segment_start = clip_index % CPS * segment
    extra_rows = jax.random.randint(jax.random.fold_in(base_key, 1), (CLIPS,), 0, segment - FRAMES + 1)
    return (segment_start + extra_rows).astype(jnp.int32)


def block_scale(own_key, dims, pieces, least, top_value):
    gain = 1.0
    for dim, parts in pieces:
        heights = jax.random.uniform(jax.random.fold_in(jax.random.fold_in(own_key, 6), dim), (parts,), jnp.float32, least / len(pieces), top_value / len(pieces))
        gain = gain * jnp.repeat(jnp.exp(heights), dims[dim] // parts).reshape((-1,) + (1,) * (len(dims) - 1 - dim))
    return gain


def noise(stream_key, extent, spread, limit, shards=(), kind=jnp.bfloat16):
    loudness = block_scale(stream_key, extent, shards, -0.22, 0.18) if shards else 1.0
    result = jax.random.normal(stream_key, extent, jnp.float32) * spread * loudness
    return jnp.minimum(jnp.maximum(result, -limit), limit).astype(kind)


def setup_inputs(seed: int = 0) -> dict:
    seeds = jax.random.split(jax.random.key(seed), 14)
    return {
        "token_gradient": noise(seeds[0], (SEQS, SEQ_LEN, HL), 1.0, 6.0, ((0, 8), (2, 4))),
        "projection": noise(seeds[1], (D, HL), HL ** -0.5, 0.0625, ((1, 4),)),
        "clip_length": draw_clip_length(jax.random.fold_in(seeds[13], 71), 0),
        "clip_offset": draw_clip_offset(jax.random.fold_in(seeds[13], 71), 0),
        "clip_home": draw_clip_home(jax.random.fold_in(seeds[13], 71), 0),
        "block_input": noise(seeds[5], (CLIPS, FRAMES, D), 1.0, 6.0, ((0, 8),)),
        "block_output": noise(seeds[6], (CLIPS, FRAMES, D), 1.0, 6.0, ((0, 8),)),
        "norm_gain": jnp.clip(1.0 + 0.18 * jax.random.normal(seeds[7], (D,), jnp.float32), 0.1, 1.9),
        "norm_bias": noise(seeds[8], (D,), 0.5, 3.0, (), jnp.float32),
        "up_weight": noise(seeds[9], (D, FF), D ** -0.5, 0.15625, ((0, 8), (1, 4))),
        "up_bias": noise(seeds[10], (FF,), 0.5, 3.0, ((0, 4),), jnp.float32),
        "down_weight": noise(seeds[11], (FF, D), FF ** -0.5, 0.078125, ((0, 4), (1, 8))),
        "post_gain": jnp.clip(1.0 + 0.18 * jax.random.normal(seeds[12], (D,), jnp.float32), 0.1, 1.9),
    }


norm_epsilon = 1e-05

def gelu_parts(pre_act):
    normal_cdf = 0.5 * (1.0 + jax.scipy.special.erf(pre_act * 0.7071067811865476))
    normal_pdf = jnp.exp(-0.5 * pre_act * pre_act) * 0.3989422804014327
    return (pre_act * normal_cdf, normal_cdf + pre_act * normal_pdf)

def norm_stats(values):
    row_mean = lax.optimization_barrier(jnp.mean(values, axis=-1, keepdims=True))
    centred = values - row_mean
    variance = lax.optimization_barrier(jnp.mean(centred * centred, axis=-1, keepdims=True))
    inverse = lax.rsqrt(variance + norm_epsilon)
    return (centred * inverse, inverse)

def norm_backward(grad_hat, normed_hat, inverse):
    first_mean = lax.optimization_barrier(jnp.mean(grad_hat, axis=-1, keepdims=True))
    second_mean = lax.optimization_barrier(jnp.mean(grad_hat * normed_hat, axis=-1, keepdims=True))
    return inverse * (grad_hat - first_mean - normed_hat * second_mean)

def row_contract(left_rows, right_rows):
    return lax.dot_general(left_rows, right_rows, (((0,), (0,)), ((), ())), preferred_element_type=jnp.float32)

def reference(token_gradient, projection, clip_length, clip_offset, clip_home, block_input, block_output, norm_gain, norm_bias, up_weight, up_bias, down_weight, post_gain):
    positions = jnp.arange(FRAMES, dtype=jnp.int32)

    def one_clip(clip_data):
        clip_index, offset, length = clip_data
        sequence = (clip_index // CPS).astype(jnp.int32)
        picked = lax.dynamic_slice(token_gradient, (sequence, offset.astype(jnp.int32), jnp.int32(0)), (1, FRAMES, HL))[0]
        picked = jnp.where((positions < length)[:, None], picked, jnp.zeros_like(picked))
        return jnp.dot(picked, projection.T, preferred_element_type=jnp.float32).astype(jnp.bfloat16)
    projected = lax.map(one_clip, (jnp.arange(CLIPS, dtype=jnp.int32), clip_offset, clip_length))
    feature_grad = jnp.zeros((CLIPS, FRAMES, D), jnp.bfloat16).at[clip_home].set(projected)
    row_total = CLIPS * FRAMES
    feature_rows = feature_grad.reshape(row_total, D).astype(jnp.float32)
    output_hat, output_inverse = norm_stats(block_output.reshape(row_total, D).astype(jnp.float32))
    post_grad = norm_backward(feature_rows * post_gain, output_hat, output_inverse)
    post_rounded = post_grad.astype(jnp.bfloat16)
    input_hat, input_inverse = norm_stats(block_input.reshape(row_total, D).astype(jnp.float32))
    normed = (input_hat * norm_gain + norm_bias).astype(jnp.bfloat16)
    pre_act = jnp.dot(normed, up_weight, preferred_element_type=jnp.float32) + up_bias
    activation, gelu_slope = gelu_parts(pre_act)
    act_rounded = activation.astype(jnp.bfloat16)
    act_grad = jnp.dot(post_rounded, down_weight.T, preferred_element_type=jnp.float32)
    pre_grad = (act_grad * gelu_slope).astype(jnp.bfloat16)
    normed_grad = jnp.dot(pre_grad, up_weight.T, preferred_element_type=jnp.float32)
    input_rows = post_grad + norm_backward(normed_grad * norm_gain, input_hat, input_inverse)
    input_gradient = input_rows.astype(jnp.bfloat16).reshape(CLIPS, FRAMES, D)
    up_gradient = row_contract(normed, pre_grad) / CLIPS
    down_gradient = row_contract(act_rounded, post_rounded) / CLIPS
    return (input_gradient, up_gradient, down_gradient)
```

```python
import jax
import jax.numpy as jnp
from jax import lax
from jax.experimental import pallas as pl
from jax.experimental.pallas import tpu as pltpu
from jax.sharding import PartitionSpec as P

CPS = 2


norm_epsilon = 1e-05


def gelu_parts(pre_act):
    normal_cdf = 0.5 * (1.0 + jax.scipy.special.erf(pre_act * 0.7071067811865476))
    normal_pdf = jnp.exp(-0.5 * pre_act * pre_act) * 0.3989422804014327
    return (pre_act * normal_cdf, normal_cdf + pre_act * normal_pdf)


def norm_stats(values):
    row_mean = jnp.mean(values, axis=-1, keepdims=True)
    centred = values - row_mean
    variance = jnp.mean(centred * centred, axis=-1, keepdims=True)
    inverse = lax.rsqrt(variance + norm_epsilon)
    return (centred * inverse, inverse)


def norm_backward(grad_hat, normed_hat, inverse):
    first_mean = jnp.mean(grad_hat, axis=-1, keepdims=True)
    second_mean = jnp.mean(grad_hat * normed_hat, axis=-1, keepdims=True)
    return inverse * (grad_hat - first_mean - normed_hat * second_mean)


def row_contract(left_rows, right_rows):
    return lax.dot_general(
        left_rows, right_rows, (((0,), (0,)), ((), ())), preferred_element_type=jnp.float32
    )


def own_columns(values, column_start, column_span):
    return lax.dynamic_slice_in_dim(values, column_start, column_span, values.ndim - 1)


def project_terms(clip_blocks, projection):
    clips_here, frames, columns = clip_blocks.shape
    flat_rows = clip_blocks.reshape(clips_here * frames, columns)
    partial_terms = lax.dot_general(
        flat_rows, projection, (((1,), (1,)), ((), ())), preferred_element_type=jnp.float32
    )
    return partial_terms.reshape(clips_here, frames, projection.shape[0])


def project_sum(clip_blocks, projection):
    return lax.psum(project_terms(clip_blocks, projection), "llm")


def deliver(clip_blocks, routing, slot_marks):
    clips_here, frames, columns = clip_blocks.shape
    devices, pair_slots, slot_count = slot_marks.shape
    packed = jnp.einsum(
        "bc,cfw->bfw", routing, clip_blocks, preferred_element_type=jnp.float32
    ).astype(jnp.bfloat16)
    packed = packed.reshape(devices, pair_slots, frames, columns)
    received, marks_in = (
        lax.all_to_all(packed, "enc", split_axis=0, concat_axis=0, tiled=True),
        lax.all_to_all(slot_marks, "enc", split_axis=0, concat_axis=0, tiled=True),
    )
    placed = jnp.einsum("npc,npfw->cfw", marks_in, received, preferred_element_type=jnp.float32)
    return placed.astype(jnp.bfloat16)


def shards(
    token_gradient,
    projection,
    clip_length,
    clip_offset,
    clip_home,
    block_input,
    block_output,
    norm_gain,
    norm_bias,
    up_weight,
    up_bias,
    down_weight,
    post_gain,
):
    devices = lax.axis_size("enc")
    clips_here, frames, model_width = block_input.shape
    pair_slots = max(1, clips_here // devices)
    positions = jnp.arange(frames, dtype=jnp.int32)
    clip_order = jnp.arange(clips_here, dtype=jnp.int32)
    target = clip_home // clips_here
    slot_place = clip_home % clips_here
    earlier = clip_order[None, :] < clip_order[:, None]
    same_target = target[None, :] == target[:, None]
    bucket_rank = jnp.sum((earlier & same_target).astype(jnp.int32), axis=1)
    bucket = target * pair_slots + bucket_rank
    buckets = jnp.arange(devices * pair_slots, dtype=jnp.int32)
    routing = (buckets[:, None] == bucket[None, :]).astype(jnp.bfloat16)
    slot_table = (slot_place[:, None] == clip_order[None, :]).astype(jnp.bfloat16)
    slot_marks = jnp.dot(routing, slot_table, preferred_element_type=jnp.float32).astype(
        jnp.bfloat16
    )
    slot_marks = slot_marks.reshape(devices, pair_slots, clips_here)

    def cut_clip(clip_index, offset, length):
        picked = lax.dynamic_slice(
            token_gradient,
            (clip_index // CPS, offset, jnp.int32(0)),
            (1, frames, token_gradient.shape[2]),
        )[0]
        return jnp.where((positions < length)[:, None], picked, jnp.zeros_like(picked))

    clip_blocks = jax.vmap(cut_clip)(clip_order, clip_offset, clip_length)
    feature_grad = project_sum(deliver(clip_blocks, routing, slot_marks), projection).astype(
        jnp.bfloat16
    )
    row_total = clips_here * frames
    feature_rows = feature_grad.reshape(row_total, model_width).astype(jnp.float32)
    output_hat, output_inverse = norm_stats(
        block_output.reshape(row_total, model_width).astype(jnp.float32)
    )
    post_grad = norm_backward(feature_rows * post_gain, output_hat, output_inverse)
    post_rounded = post_grad.astype(jnp.bfloat16)
    input_hat, input_inverse = norm_stats(
        block_input.reshape(row_total, model_width).astype(jnp.float32)
    )
    normed = (input_hat * norm_gain + norm_bias).astype(jnp.bfloat16)
    up_full, down_full = (
        lax.all_gather(up_weight, "enc", axis=0, tiled=True),
        lax.all_gather(down_weight, "enc", axis=1, tiled=True),
    )
    pre_act = jnp.dot(normed, up_full, preferred_element_type=jnp.float32) + up_bias
    activation, gelu_slope = gelu_parts(pre_act)
    act_rounded = activation.astype(jnp.bfloat16)
    act_grad = lax.dot_general(
        post_rounded, down_full, (((1,), (1,)), ((), ())), preferred_element_type=jnp.float32
    )
    pre_grad = (act_grad * gelu_slope).astype(jnp.bfloat16)
    normed_part = lax.dot_general(
        pre_grad, up_full, (((1,), (1,)), ((), ())), preferred_element_type=jnp.float32
    )
    groups = lax.axis_size("llm")
    share_width = model_width // groups
    share_start = lax.axis_index("llm") * share_width
    normed_grad = lax.psum(normed_part, "llm")
    full_grad = post_grad + norm_backward(normed_grad * norm_gain, input_hat, input_inverse)
    input_rows = own_columns(full_grad, share_start, share_width)
    input_gradient = input_rows.astype(jnp.bfloat16).reshape(clips_here, frames, share_width)
    scale_count = clips_here * devices
    up_gradient = (
        lax.psum_scatter(
            row_contract(
                own_columns(normed, jnp.int32(0), up_weight.shape[0] * lax.axis_size("enc")),
                pre_grad,
            ),
            "enc",
            scatter_dimension=0,
            tiled=True,
        )
        / scale_count
    )
    down_gradient = (
        lax.psum_scatter(
            row_contract(
                own_columns(
                    post_rounded, jnp.int32(0), down_weight.shape[1] * lax.axis_size("enc")
                ),
                act_rounded,
            ),
            "enc",
            scatter_dimension=0,
            tiled=True,
        )
        / scale_count
    ).T
    return (input_gradient, up_gradient, down_gradient)


MESH = pl.DeviceIdType.MESH
BF = jnp.bfloat16
F32 = jnp.float32

W_Z = 0
W_S = 6
MARK = 14
RS1 = 21
EXCH = 24
AG = 31
GS = 34
GZ = 42
RS2 = 48
FIN = 51
COPIES = 54


def dot(left, right, left_dim, right_dim):
    return lax.dot_general(
        left, right, (((left_dim,), (right_dim,)), ((), ())), preferred_element_type=F32
    )


def fused_kernel(
    clips_ref,
    proj_ref,
    marks_ref,
    block_in_ref,
    block_out_ref,
    gain_ref,
    bias_ref,
    post_gain_ref,
    up_bias_ref,
    up_ref,
    down_ref,
    input_out,
    up_out,
    down_out,
    weights,
    marks_in,
    rs1_send,
    rs1_recv,
    exch_send,
    exch_recv,
    feat,
    normed,
    normed_t,
    post,
    post_t,
    act,
    slope,
    pre_grad,
    rs2_send,
    rs2_recv,
    grad_own,
    gs_send,
    gs_recv,
    gz_send,
    gz_recv,
    fin_send,
    send_sems,
    recv_sems,
):
    l = lax.axis_index("llm")
    e = lax.axis_index("enc")
    z = e // 2
    c = e % 2
    other = z * 2 + 1 - c
    width = up_ref.shape[1]
    depth = proj_ref.shape[0]
    part = up_ref.shape[0]
    rows = clips_ref.shape[0]
    own = rows // 4
    tile = 256
    chunk = 64
    scale = 1.0 / (8 * 16)

    def copy(src, dst, index, device):
        return pltpu.make_async_remote_copy(
            src_ref=src,
            dst_ref=dst,
            send_sem=send_sems.at[index],
            recv_sem=recv_sems.at[index],
            device_id=device,
            device_id_type=MESH,
        )

    barrier = pltpu.get_barrier_semaphore()
    for k in range(1, 4):
        pl.semaphore_signal(barrier, inc=1, device_id=((l + k) % 4, e), device_id_type=MESH)
    for k in range(1, 8):
        pl.semaphore_signal(barrier, inc=1, device_id=(l, (e + k) % 8), device_id_type=MESH)
    pl.semaphore_wait(barrier, 10)

    sent = []

    def start(*args):
        one = copy(*args)
        one.start()
        sent.append(one)
        return one

    mark_copies = [
        start(marks_ref.at[(e + k) % 8], marks_in.at[e], MARK + k - 1, (l, (e + k) % 8))
        for k in range(1, 8)
    ]
    marks_in[e] = marks_ref[e]
    z_copies = []
    own_copies = []
    for kind, ref in enumerate((up_ref, down_ref)):
        z_copies.append(
            [
                start(
                    ref,
                    weights.at[kind, e],
                    W_Z + 3 * kind + k - 1,
                    (l, ((z + k) % 4) * 2 + c),
                )
                for k in range(1, 4)
            ]
        )
        own_copies.append(start(ref, weights.at[kind, e], W_S + 4 * kind, (l, other)))
        weights[kind, e] = ref[...]

    @pl.loop(0, depth // tile)
    def _(t):
        columns = pl.ds(pl.multiple_of(t * tile, tile), tile)
        rs1_send[:, columns] = dot(clips_ref[...], proj_ref[columns, :], 1, 1).astype(BF)

    def rows_of(index):
        return pl.ds(pl.multiple_of(index * own, own), own)

    rs1_copies = [
        start(rs1_send.at[rows_of((l + k) % 4), :], rs1_recv.at[k - 1], RS1 + k - 1, ((l + k) % 4, e))
        for k in range(1, 4)
    ]

    @pl.loop(0, rows // chunk)
    def _(t):
        at = pl.ds(pl.multiple_of(t * chunk, chunk), chunk)
        hat, _ = norm_stats(block_in_ref[at, :].astype(F32))
        normed[at, :] = (hat * gain_ref[...] + bias_ref[...]).astype(BF)

    @pl.loop(0, depth // 128)
    def _(t):
        at = pl.ds(pl.multiple_of(t * 128, 128), 128)
        normed_t[at, :] = normed[:, at].T

    for one in rs1_copies:
        one.wait_recv()
    total = rs1_send[rows_of(l), :].astype(F32)
    for k in range(3):
        total += rs1_recv[k].astype(F32)
    exch_send[...] = total.astype(BF).reshape(exch_send.shape)
    exch_copies = [
        start(exch_send.at[(e + k) % 8], exch_recv.at[e], EXCH + k - 1, (l, (e + k) % 8))
        for k in range(1, 8)
    ]
    exch_recv[e] = exch_send[e]
    for one in mark_copies:
        one.wait_recv()
    for one in exch_copies:
        one.wait_recv()
    feat[rows_of(l), :] = dot(
        marks_in[...].reshape(own, own), exch_recv[...].reshape(own, depth), 0, 0
    ).astype(BF)
    ag_copies = [
        start(feat.at[rows_of(l), :], feat.at[rows_of(l), :], AG + k - 1, ((l + k) % 4, e))
        for k in range(1, 4)
    ]

    def gather_weight(kind):
        passed = [own_copies[kind]]
        for k in range(1, 4):
            z_copies[kind][k - 1].wait_recv()
            block = weights.at[kind, ((z - k + 4) % 4) * 2 + c]
            passed.append(start(block, block, W_S + 4 * kind + k, (l, other)))
        for one in passed:
            one.wait_recv()

    def whole(kind):
        return weights[kind].reshape(depth, width)

    gather_weight(0)

    @pl.loop(0, width // tile)
    def _(t):
        at = pl.ds(pl.multiple_of(t * tile, tile), tile)
        up_tile = weights[0, :, :, at].reshape(depth, tile)
        pre_act = dot(normed[...], up_tile, 1, 0) + up_bias_ref[:, at]
        activation, gelu_slope = gelu_parts(pre_act)
        act[:, at] = activation.astype(BF)
        slope[:, at] = gelu_slope

    def post_rows(at):
        hat, inverse = norm_stats(block_out_ref[at, :].astype(F32))
        return norm_backward(feat[at, :].astype(F32) * post_gain_ref[...], hat, inverse)

    for one in ag_copies:
        one.wait_recv()

    @pl.loop(0, rows // chunk)
    def _(t):
        at = pl.ds(pl.multiple_of(t * chunk, chunk), chunk)
        post[at, :] = post_rows(at).astype(BF)

    @pl.loop(0, depth // 128)
    def _(t):
        at = pl.ds(pl.multiple_of(t * 128, 128), 128)
        post_t[at, :] = post[:, at].T

    def weight_terms(kind, left_t, right):
        def term(block):
            left = left_t[pl.ds(pl.multiple_of(block * part, part), part), :]
            return dot(left, right[...], 1, 0)

        copies = []
        for k in range(4):
            zk = (z + k) % 4
            gs_send[kind, k] = term(zk * 2 + 1 - c).astype(BF)
            copies.append(
                start(gs_send.at[kind, k], gs_recv.at[kind, k], GS + 4 * kind + k, (l, other))
            )
        for k in range(4):
            zk = (z + k) % 4
            grad_own[kind, k] = term(zk * 2 + c)
        return copies

    def weight_sums(kind, copies):
        sums = []
        for k in (1, 2, 3):
            copies[k].wait_recv()
            both = grad_own[kind, k] + gs_recv[kind, k].astype(F32)
            gz_send[kind, k - 1] = both.astype(BF)
            sums.append(
                start(
                    gz_send.at[kind, k - 1],
                    gz_recv.at[kind, k - 1],
                    GZ + 3 * kind + k - 1,
                    (l, ((z + k) % 4) * 2 + c),
                )
            )
        copies[0].wait_recv()
        return sums

    def weight_result(kind, sums, out):
        for one in sums:
            one.wait_recv()
        total = grad_own[kind, 0] + gs_recv[kind, 0].astype(F32)
        for k in range(3):
            total += gz_recv[kind, k].astype(F32)
        out[...] = total * scale

    down_copies = weight_terms(1, post_t, act)
    down_sums = weight_sums(1, down_copies)

    gather_weight(1)

    @pl.loop(0, width // tile)
    def _(t):
        at = pl.ds(pl.multiple_of(t * tile, tile), tile)
        down_tile = weights[1, :, :, at].reshape(depth, tile)
        pre_grad[:, at] = (dot(post[...], down_tile, 1, 0) * slope[:, at]).astype(BF)

    up_copies = weight_terms(0, normed_t, pre_grad)
    up_sums = weight_sums(0, up_copies)

    for k in range(8):
        rs2_send[:, k * part : (k + 1) * part] = dot(pre_grad[...], weights[0, k], 1, 1).astype(BF)
    rs2_copies = [
        start(rs2_send.at[rows_of((l + k) % 4), :], rs2_recv.at[k - 1], RS2 + k - 1, ((l + k) % 4, e))
        for k in range(1, 4)
    ]
    for one in rs2_copies:
        one.wait_recv()
    normed_grad = rs2_send[rows_of(l), :].astype(F32)
    for k in range(3):
        normed_grad += rs2_recv[k].astype(F32)
    hat, inverse = norm_stats(block_in_ref[rows_of(l), :].astype(F32))
    result = post_rows(rows_of(l)) + norm_backward(normed_grad * gain_ref[...], hat, inverse)
    share = depth // 4
    for j in range(4):
        fin_send[j] = result[:, j * share : (j + 1) * share].astype(BF)
    fin_copies = [
        start(fin_send.at[(l + k) % 4], input_out.at[l], FIN + k - 1, ((l + k) % 4, e))
        for k in range(1, 4)
    ]
    input_out[l] = fin_send[l]

    weight_result(1, down_sums, down_out)
    weight_result(0, up_sums, up_out)
    for one in fin_copies:
        one.wait_recv()
    for one in sent:
        one.wait_send()


def fused_shards(
    token_gradient,
    projection,
    clip_length,
    clip_offset,
    clip_home,
    block_input,
    block_output,
    norm_gain,
    norm_bias,
    up_weight,
    up_bias,
    down_weight,
    post_gain,
):
    groups = lax.axis_size("llm")
    devices = lax.axis_size("enc")
    clips_here, frames, depth = block_input.shape
    sequences, sequence_rows, columns = token_gradient.shape
    pair_slots = clips_here // devices
    rows = clips_here * frames
    piece = frames // groups
    own = rows // groups
    clip_order = jnp.arange(clips_here, dtype=jnp.int32)
    target = clip_home // clips_here
    slot_place = clip_home % clips_here
    earlier = clip_order[None, :] < clip_order[:, None]
    same_target = target[None, :] == target[:, None]
    bucket_rank = jnp.sum((earlier & same_target).astype(jnp.int32), axis=1)
    bucket = target * pair_slots + bucket_rank
    in_bucket = (clip_order[:, None] == bucket[None, :]).astype(jnp.int32)

    def by_bucket(values):
        return jnp.sum(in_bucket * values[None, :], axis=1)

    first_row = by_bucket((clip_order // CPS) * sequence_rows + clip_offset)
    lengths = by_bucket(clip_length)
    places = by_bucket(slot_place)
    frame = jnp.arange(frames, dtype=jnp.int32).reshape(groups, 1, piece)
    source = jnp.where(
        frame < lengths[None, :, None], first_row[None, :, None] + frame, -1
    ).reshape(rows)
    token_rows = jnp.arange(sequences * sequence_rows, dtype=jnp.int32)
    picks = (source[:, None] == token_rows[None, :]).astype(BF)
    clips = jnp.dot(
        picks,
        token_gradient.reshape(sequences * sequence_rows, columns),
        preferred_element_type=F32,
    ).astype(BF)
    goal = (places[:, None] * piece + jnp.arange(piece, dtype=jnp.int32)[None, :]).reshape(own)
    marks = (goal[:, None] == jnp.arange(own, dtype=jnp.int32)[None, :]).astype(BF)
    marks = marks.reshape(devices, pair_slots * piece, own)

    def by_part(values):
        return (
            values.reshape(clips_here, groups, piece, depth).swapaxes(0, 1).reshape(rows, depth)
        )

    part, width = up_weight.shape
    share = depth // groups
    vmem = pl.BlockSpec(memory_space=pltpu.VMEM)
    exchange = (devices, own // devices, depth)
    input_parts, up_gradient, down_gradient = pl.pallas_call(
        fused_kernel,
        out_shape=(
            jax.ShapeDtypeStruct((groups, own, share), BF),
            jax.ShapeDtypeStruct((part, width), F32),
            jax.ShapeDtypeStruct((part, width), F32),
        ),
        in_specs=[vmem] * 11,
        out_specs=(vmem, vmem, vmem),
        scratch_shapes=[
            pltpu.VMEM((2, devices, part, width), BF),
            pltpu.VMEM(marks.shape, BF),
            pltpu.VMEM((rows, depth), BF),
            pltpu.VMEM((3, own, depth), BF),
            pltpu.VMEM(exchange, BF),
            pltpu.VMEM(exchange, BF),
            pltpu.VMEM((rows, depth), BF),
            pltpu.VMEM((rows, depth), BF),
            pltpu.VMEM((depth, rows), BF),
            pltpu.VMEM((rows, depth), BF),
            pltpu.VMEM((depth, rows), BF),
            pltpu.VMEM((rows, width), BF),
            pltpu.VMEM((rows, width), F32),
            pltpu.VMEM((rows, width), BF),
            pltpu.VMEM((rows, depth), BF),
            pltpu.VMEM((3, own, depth), BF),
            pltpu.VMEM((2, 4, part, width), F32),
            pltpu.VMEM((2, 4, part, width), BF),
            pltpu.VMEM((2, 4, part, width), BF),
            pltpu.VMEM((2, 3, part, width), BF),
            pltpu.VMEM((2, 3, part, width), BF),
            pltpu.VMEM((groups, own, share), BF),
            pltpu.SemaphoreType.DMA((COPIES,)),
            pltpu.SemaphoreType.DMA((COPIES,)),
        ],
        compiler_params=pltpu.CompilerParams(
            collective_id=0, has_side_effects=True, vmem_limit_bytes=62 * 1024 * 1024
        ),
    )(
        clips,
        projection,
        marks,
        by_part(block_input),
        by_part(block_output),
        norm_gain.reshape(1, depth),
        norm_bias.reshape(1, depth),
        post_gain.reshape(1, depth),
        up_bias.reshape(1, width),
        up_weight,
        down_weight.T,
    )
    input_gradient = (
        input_parts.reshape(groups, clips_here, piece, share)
        .swapaxes(0, 1)
        .reshape(clips_here, frames, share)
    )
    return (input_gradient, up_gradient, down_gradient.T)


def solution(mesh):
    fused = mesh.shape["llm"] == 4 and mesh.shape["enc"] == 8
    return jax.shard_map(
        fused_shards if fused else shards,
        mesh=mesh,
        in_specs=(
            P("enc", None, "llm"),
            P(None, "llm"),
            P("enc"),
            P("enc"),
            P("enc"),
            P("enc", None, None),
            P("enc", None, None),
            P(),
            P(),
            P("enc", "llm"),
            P("llm"),
            P("llm", "enc"),
            P(),
        ),
        out_specs=(P("enc", None, "llm"), P("enc", "llm"), P("llm", "enc")),
        check_vma=False,
    )
```

```python
import jax
import jax.numpy as jnp
from jax import lax
from jax.experimental import pallas as pl
from jax.experimental.pallas import tpu as pltpu
from jax.sharding import PartitionSpec as P

CPS = 2


norm_epsilon = 1e-05


def gelu_parts(pre_act):
    normal_cdf = 0.5 * (1.0 + jax.scipy.special.erf(pre_act * 0.7071067811865476))
    normal_pdf = jnp.exp(-0.5 * pre_act * pre_act) * 0.3989422804014327
    return (pre_act * normal_cdf, normal_cdf + pre_act * normal_pdf)


def norm_stats(values):
    row_mean = jnp.mean(values, axis=-1, keepdims=True)
    centred = values - row_mean
    variance = jnp.mean(centred * centred, axis=-1, keepdims=True)
    inverse = lax.rsqrt(variance + norm_epsilon)
    return (centred * inverse, inverse)


def norm_backward(grad_hat, normed_hat, inverse):
    first_mean = jnp.mean(grad_hat, axis=-1, keepdims=True)
    second_mean = jnp.mean(grad_hat * normed_hat, axis=-1, keepdims=True)
    return inverse * (grad_hat - first_mean - normed_hat * second_mean)


def row_contract(left_rows, right_rows):
    return lax.dot_general(
        left_rows, right_rows, (((0,), (0,)), ((), ())), preferred_element_type=jnp.float32
    )


def own_columns(values, column_start, column_span):
    return lax.dynamic_slice_in_dim(values, column_start, column_span, values.ndim - 1)


def project_terms(clip_blocks, projection):
    clips_here, frames, columns = clip_blocks.shape
    flat_rows = clip_blocks.reshape(clips_here * frames, columns)
    partial_terms = lax.dot_general(
        flat_rows, projection, (((1,), (1,)), ((), ())), preferred_element_type=jnp.float32
    )
    return partial_terms.reshape(clips_here, frames, projection.shape[0])


def project_sum(clip_blocks, projection):
    return lax.psum(project_terms(clip_blocks, projection), "llm")


def deliver(clip_blocks, routing, slot_marks):
    clips_here, frames, columns = clip_blocks.shape
    devices, pair_slots, slot_count = slot_marks.shape
    packed = jnp.einsum(
        "bc,cfw->bfw", routing, clip_blocks, preferred_element_type=jnp.float32
    ).astype(jnp.bfloat16)
    packed = packed.reshape(devices, pair_slots, frames, columns)
    received, marks_in = (
        lax.all_to_all(packed, "enc", split_axis=0, concat_axis=0, tiled=True),
        lax.all_to_all(slot_marks, "enc", split_axis=0, concat_axis=0, tiled=True),
    )
    placed = jnp.einsum("npc,npfw->cfw", marks_in, received, preferred_element_type=jnp.float32)
    return placed.astype(jnp.bfloat16)


def shards(
    token_gradient,
    projection,
    clip_length,
    clip_offset,
    clip_home,
    block_input,
    block_output,
    norm_gain,
    norm_bias,
    up_weight,
    up_bias,
    down_weight,
    post_gain,
):
    devices = lax.axis_size("enc")
    clips_here, frames, model_width = block_input.shape
    pair_slots = max(1, clips_here // devices)
    positions = jnp.arange(frames, dtype=jnp.int32)
    clip_order = jnp.arange(clips_here, dtype=jnp.int32)
    target = clip_home // clips_here
    slot_place = clip_home % clips_here
    earlier = clip_order[None, :] < clip_order[:, None]
    same_target = target[None, :] == target[:, None]
    bucket_rank = jnp.sum((earlier & same_target).astype(jnp.int32), axis=1)
    bucket = target * pair_slots + bucket_rank
    buckets = jnp.arange(devices * pair_slots, dtype=jnp.int32)
    routing = (buckets[:, None] == bucket[None, :]).astype(jnp.bfloat16)
    slot_table = (slot_place[:, None] == clip_order[None, :]).astype(jnp.bfloat16)
    slot_marks = jnp.dot(routing, slot_table, preferred_element_type=jnp.float32).astype(
        jnp.bfloat16
    )
    slot_marks = slot_marks.reshape(devices, pair_slots, clips_here)

    def cut_clip(clip_index, offset, length):
        picked = lax.dynamic_slice(
            token_gradient,
            (clip_index // CPS, offset, jnp.int32(0)),
            (1, frames, token_gradient.shape[2]),
        )[0]
        return jnp.where((positions < length)[:, None], picked, jnp.zeros_like(picked))

    clip_blocks = jax.vmap(cut_clip)(clip_order, clip_offset, clip_length)
    feature_grad = project_sum(deliver(clip_blocks, routing, slot_marks), projection).astype(
        jnp.bfloat16
    )
    row_total = clips_here * frames
    feature_rows = feature_grad.reshape(row_total, model_width).astype(jnp.float32)
    output_hat, output_inverse = norm_stats(
        block_output.reshape(row_total, model_width).astype(jnp.float32)
    )
    post_grad = norm_backward(feature_rows * post_gain, output_hat, output_inverse)
    post_rounded = post_grad.astype(jnp.bfloat16)
    input_hat, input_inverse = norm_stats(
        block_input.reshape(row_total, model_width).astype(jnp.float32)
    )
    normed = (input_hat * norm_gain + norm_bias).astype(jnp.bfloat16)
    up_full, down_full = (
        lax.all_gather(up_weight, "enc", axis=0, tiled=True),
        lax.all_gather(down_weight, "enc", axis=1, tiled=True),
    )
    pre_act = jnp.dot(normed, up_full, preferred_element_type=jnp.float32) + up_bias
    activation, gelu_slope = gelu_parts(pre_act)
    act_rounded = activation.astype(jnp.bfloat16)
    act_grad = lax.dot_general(
        post_rounded, down_full, (((1,), (1,)), ((), ())), preferred_element_type=jnp.float32
    )
    pre_grad = (act_grad * gelu_slope).astype(jnp.bfloat16)
    normed_part = lax.dot_general(
        pre_grad, up_full, (((1,), (1,)), ((), ())), preferred_element_type=jnp.float32
    )
    groups = lax.axis_size("llm")
    share_width = model_width // groups
    share_start = lax.axis_index("llm") * share_width
    normed_grad = lax.psum(normed_part, "llm")
    full_grad = post_grad + norm_backward(normed_grad * norm_gain, input_hat, input_inverse)
    input_rows = own_columns(full_grad, share_start, share_width)
    input_gradient = input_rows.astype(jnp.bfloat16).reshape(clips_here, frames, share_width)
    scale_count = clips_here * devices
    up_gradient = (
        lax.psum_scatter(
            row_contract(
                own_columns(normed, jnp.int32(0), up_weight.shape[0] * lax.axis_size("enc")),
                pre_grad,
            ),
            "enc",
            scatter_dimension=0,
            tiled=True,
        )
        / scale_count
    )
    down_gradient = (
        lax.psum_scatter(
            row_contract(
                own_columns(
                    post_rounded, jnp.int32(0), down_weight.shape[1] * lax.axis_size("enc")
                ),
                act_rounded,
            ),
            "enc",
            scatter_dimension=0,
            tiled=True,
        )
        / scale_count
    ).T
    return (input_gradient, up_gradient, down_gradient)


MESH = pl.DeviceIdType.MESH
BF = jnp.bfloat16
F32 = jnp.float32

W_RIGHT = 0
W_LEFT = 8
W_S = 16
MARK = 24
RS1 = 31
EXCH = 34
AG = 41
GS = 44
C_RIGHT = 52
C_LEFT = 60
RS2 = 68
FIN = 71
COPIES = 74


def dot(left, right, left_dim, right_dim):
    return lax.dot_general(
        left, right, (((left_dim,), (right_dim,)), ((), ())), preferred_element_type=F32
    )


def fused_kernel(
    tokens_hbm,
    source_ref,
    proj_hbm,
    marks_ref,
    block_in_ref,
    block_out_ref,
    vectors_ref,
    up_ref,
    down_ref,
    input_out,
    up_out,
    down_out,
    tokens_ref,
    proj_ref,
    clips_ref,
    weights,
    marks_in,
    rs1_send,
    rs1_recv,
    exch_send,
    exch_recv,
    feat,
    normed,
    normed_t,
    post,
    post_t,
    act,
    slope,
    pre_grad,
    rs2_recv,
    grad_own,
    gs_send,
    gs_recv,
    chain_send,
    chain_recv,
    fin_send,
    load_sems,
    send_sems,
    recv_sems,
):
    l = lax.axis_index("llm")
    e = lax.axis_index("enc")
    z = e // 2
    c = e % 2
    other = z * 2 + 1 - c
    width = up_ref.shape[1]
    depth = proj_ref.shape[0]
    part = up_ref.shape[0]
    rows = clips_ref.shape[0]
    own = rows // 4
    tile = 256
    chunk = 64
    scale = 1.0 / (8 * 16)

    def copy(src, dst, index, device):
        return pltpu.make_async_remote_copy(
            src_ref=src,
            dst_ref=dst,
            send_sem=send_sems.at[index],
            recv_sem=recv_sems.at[index],
            device_id=device,
            device_id_type=MESH,
        )

    loads = [
        pltpu.make_async_copy(tokens_hbm, tokens_ref, load_sems.at[0]),
        pltpu.make_async_copy(proj_hbm, proj_ref, load_sems.at[1]),
    ]
    for one in loads:
        one.start()
    gain = vectors_ref[0:1, :]
    bias = vectors_ref[1:2, :]
    post_gain = vectors_ref[2:3, :]

    barrier = pltpu.get_barrier_semaphore()
    for k in range(1, 4):
        pl.semaphore_signal(barrier, inc=1, device_id=((l + k) % 4, e), device_id_type=MESH)
    for k in range(1, 8):
        pl.semaphore_signal(barrier, inc=1, device_id=(l, (e + k) % 8), device_id_type=MESH)
    pl.semaphore_wait(barrier, 10)

    sent = []

    def start(*args):
        one = copy(*args)
        one.start()
        sent.append(one)
        return one

    def device_at(z_to):
        return (l, z_to * 2 + c)

    def pass_block(kind, block_z, step, action):
        block = weights.at[kind, block_z * 2 + c]

        def over(index, device):
            return copy(block, block, index + 4 * kind + block_z, device)

        across = over(W_S, (l, other))

        def along(index, z_to):
            if action == "send":
                over(index, device_at(z_to)).start()
            else:
                over(index, device_at(z_to)).wait_send()

        if action == "send":
            across.start()
        else:
            across.wait_send()
        return along, over

    def hop(kind, step, action="send"):
        if step == 0:
            along, _ = pass_block(kind, z, 0, action)

            @pl.when(z < 3)
            def _():
                along(W_RIGHT, z + 1)

            @pl.when(z > 0)
            def _():
                along(W_LEFT, z - 1)

            return

        @pl.when(z >= step)
        def _():
            block_z = z - step
            if action == "send":
                block = weights.at[kind, block_z * 2 + c]
                copy(block, block, W_RIGHT + 4 * kind + block_z, device_at(z - 1)).wait_recv()
            along, _ = pass_block(kind, block_z, step, action)

            @pl.when(z < 3)
            def _():
                along(W_RIGHT, z + 1)

        @pl.when(z + step <= 3)
        def _():
            block_z = z + step
            if action == "send":
                block = weights.at[kind, block_z * 2 + c]
                copy(block, block, W_LEFT + 4 * kind + block_z, device_at(z + 1)).wait_recv()
            along, _ = pass_block(kind, block_z, step, action)

            @pl.when(z > 0)
            def _():
                along(W_LEFT, z - 1)

    def whole_weight(kind):
        for block_z in range(4):
            block = weights.at[kind, block_z * 2 + 1 - c]
            copy(block, block, W_S + 4 * kind + block_z, (l, other)).wait_recv()

    weights[0, e] = up_ref[...]
    hop(0, 0)
    mark_copies = [
        start(marks_ref.at[(e + k) % 8], marks_in.at[e], MARK + k - 1, (l, (e + k) % 8))
        for k in range(1, 8)
    ]
    marks_in[e] = marks_ref[e]
    weights[1, e] = down_ref[...]

    token_rows = tokens_ref.shape[0]
    order = lax.broadcasted_iota(jnp.int32, (rows, token_rows), 1)
    act[:, :token_rows] = jnp.where(source_ref[...] == order, 1.0, 0.0).astype(BF)
    loads[0].wait()

    @pl.loop(0, clips_ref.shape[1] // tile)
    def _(t):
        columns = pl.ds(pl.multiple_of(t * tile, tile), tile)
        clips_ref[:, columns] = dot(act[:, :token_rows], tokens_ref[:, columns], 1, 0).astype(BF)

    loads[1].wait()

    @pl.loop(0, depth // tile)
    def _(t):
        columns = pl.ds(pl.multiple_of(t * tile, tile), tile)
        rs1_send[:, columns] = dot(clips_ref[...], proj_ref[columns, :], 1, 1).astype(BF)

    def rows_of(index):
        return pl.ds(pl.multiple_of(index * own, own), own)

    rs1_copies = [
        start(rs1_send.at[rows_of((l + k) % 4), :], rs1_recv.at[k - 1], RS1 + k - 1, ((l + k) % 4, e))
        for k in range(1, 4)
    ]

    @pl.loop(0, rows // chunk)
    def _(t):
        at = pl.ds(pl.multiple_of(t * chunk, chunk), chunk)
        hat, _ = norm_stats(block_in_ref[at, :].astype(F32))
        normed[at, :] = (hat * gain + bias).astype(BF)

    @pl.loop(0, depth // 128)
    def _(t):
        at = pl.ds(pl.multiple_of(t * 128, 128), 128)
        normed_t[at, :] = normed[:, at].T

    hop(0, 1)
    hop(1, 0)
    for one in rs1_copies:
        one.wait_recv()
    total = rs1_send[rows_of(l), :].astype(F32)
    for k in range(3):
        total += rs1_recv[k].astype(F32)
    exch_send[...] = total.astype(BF).reshape(exch_send.shape)
    exch_copies = [
        start(exch_send.at[(e + k) % 8], exch_recv.at[e], EXCH + k - 1, (l, (e + k) % 8))
        for k in range(1, 8)
    ]
    exch_recv[e] = exch_send[e]
    hop(0, 2)
    for one in mark_copies:
        one.wait_recv()
    for one in exch_copies:
        one.wait_recv()
    feat[rows_of(l), :] = dot(
        marks_in[...].reshape(own, own), exch_recv[...].reshape(own, depth), 0, 0
    ).astype(BF)
    ag_copies = [
        start(feat.at[rows_of(l), :], feat.at[rows_of(l), :], AG + k - 1, ((l + k) % 4, e))
        for k in range(1, 4)
    ]

    hop(1, 1)
    hop(0, 3)
    whole_weight(0)

    @pl.loop(0, width // tile)
    def _(t):
        at = pl.ds(pl.multiple_of(t * tile, tile), tile)
        up_tile = weights[0, :, :, at].reshape(depth, tile)
        pre_act = dot(normed[...], up_tile, 1, 0) + vectors_ref[3:4, at]
        activation, gelu_slope = gelu_parts(pre_act)
        act[:, at] = activation.astype(BF)
        slope[:, at] = gelu_slope

    def post_rows(at):
        hat, inverse = norm_stats(block_out_ref[at, :].astype(F32))
        return norm_backward(feat[at, :].astype(F32) * post_gain, hat, inverse)

    hop(1, 2)
    for one in ag_copies:
        one.wait_recv()

    @pl.loop(0, rows // chunk)
    def _(t):
        at = pl.ds(pl.multiple_of(t * chunk, chunk), chunk)
        post[at, :] = post_rows(at).astype(BF)

    @pl.loop(0, depth // 128)
    def _(t):
        at = pl.ds(pl.multiple_of(t * 128, 128), 128)
        post_t[at, :] = post[:, at].T

    def weight_terms(kind, left_t, right):
        def term(block):
            left = left_t[pl.ds(pl.multiple_of(block * part, part), part), :]
            return dot(left, right[...], 1, 0)

        copies = []
        for k in range(4):
            gs_send[kind, k] = term(k * 2 + 1 - c).astype(BF)
            copies.append(
                start(gs_send.at[kind, k], gs_recv.at[kind, k], GS + 4 * kind + k, (l, other))
            )
        for k in range(4):
            grad_own[kind, k] = term(k * 2 + c)
        for one in copies:
            one.wait_recv()

    def chain_copy(kind, to_z, step):
        slot = jnp.where(to_z == z + step, 4, to_z) if step < 0 else to_z
        return copy(
            chain_send.at[kind, to_z],
            chain_recv.at[kind, slot],
            (C_RIGHT if step > 0 else C_LEFT) + 4 * kind + to_z,
            device_at(z + step),
        )

    def received(kind, to_z, step):
        slot = jnp.where(to_z == z, 4, to_z) if step < 0 else to_z
        block = chain_recv.at[kind, slot]
        index = (C_RIGHT if step > 0 else C_LEFT) + 4 * kind + to_z
        copy(block, block, index, device_at(z - step)).wait_recv()
        return chain_recv[kind, slot].astype(F32)

    def chain_ends(kind):
        def send(to_z, step):
            total = grad_own[kind, to_z] + gs_recv[kind, to_z].astype(F32)
            chain_send[kind, to_z] = total.astype(BF)
            chain_copy(kind, to_z, step).start()

        @pl.when(z == 0)
        def _():
            for to_z in (3, 2, 1):
                send(to_z, 1)

        @pl.when(z == 3)
        def _():
            for to_z in (0, 1, 2):
                send(to_z, -1)

    def chain_middle(kind):
        def send(to_z, step):
            total = grad_own[kind, to_z] + gs_recv[kind, to_z].astype(F32)
            chain_send[kind, to_z] = (total + received(kind, to_z, step)).astype(BF)
            chain_copy(kind, to_z, step).start()

        @pl.when(z == 1)
        def _():
            send(3, 1)
            send(2, 1)
            send(0, -1)

        @pl.when(z == 2)
        def _():
            send(0, -1)
            send(1, -1)
            send(3, 1)

    def weight_result(kind, out):
        out[...] = grad_own[kind, z] + gs_recv[kind, z].astype(F32)

        @pl.when(z > 0)
        def _():
            out[...] += received(kind, z, 1)

        @pl.when(z < 3)
        def _():
            out[...] += received(kind, z, -1)

        out[...] *= scale

    def chain_done(kind):
        for to_z in range(4):

            @pl.when(z < to_z)
            def _():
                chain_copy(kind, to_z, 1).wait_send()

            @pl.when(z > to_z)
            def _():
                chain_copy(kind, to_z, -1).wait_send()

    weight_terms(1, post_t, act)
    chain_ends(1)
    hop(1, 3)
    whole_weight(1)

    @pl.loop(0, width // tile)
    def _(t):
        at = pl.ds(pl.multiple_of(t * tile, tile), tile)
        down_tile = weights[1, :, :, at].reshape(depth, tile)
        pre_grad[:, at] = (dot(post[...], down_tile, 1, 0) * slope[:, at]).astype(BF)

    weight_terms(0, normed_t, pre_grad)
    chain_ends(0)
    for one in rs1_copies:
        one.wait_send()
    sent[:] = [one for one in sent if not any(one is early for early in rs1_copies)]
    rs2_send = rs1_send
    for k in range(8):
        rs2_send[:, k * part : (k + 1) * part] = dot(pre_grad[...], weights[0, k], 1, 1).astype(BF)
    rs2_copies = [
        start(rs2_send.at[rows_of((l + k) % 4), :], rs2_recv.at[k - 1], RS2 + k - 1, ((l + k) % 4, e))
        for k in range(1, 4)
    ]
    chain_middle(1)
    for one in rs2_copies:
        one.wait_recv()
    normed_grad = rs2_send[rows_of(l), :].astype(F32)
    for k in range(3):
        normed_grad += rs2_recv[k].astype(F32)
    hat, inverse = norm_stats(block_in_ref[rows_of(l), :].astype(F32))
    result = post_rows(rows_of(l)) + norm_backward(normed_grad * gain, hat, inverse)
    share = depth // 4
    for j in range(4):
        fin_send[j] = result[:, j * share : (j + 1) * share].astype(BF)
    fin_copies = [
        start(fin_send.at[(l + k) % 4], input_out.at[l], FIN + k - 1, ((l + k) % 4, e))
        for k in range(1, 4)
    ]
    input_out[l] = fin_send[l]

    chain_middle(0)
    weight_result(1, down_out)
    weight_result(0, up_out)
    for one in fin_copies:
        one.wait_recv()
    for one in sent:
        one.wait_send()
    for kind in range(2):
        for step in range(4):
            hop(kind, step, "wait")
        chain_done(kind)


def fused_shards(
    token_gradient,
    projection,
    clip_length,
    clip_offset,
    clip_home,
    block_input,
    block_output,
    norm_gain,
    norm_bias,
    up_weight,
    up_bias,
    down_weight,
    post_gain,
):
    groups = lax.axis_size("llm")
    devices = lax.axis_size("enc")
    clips_here, frames, depth = block_input.shape
    sequences, sequence_rows, columns = token_gradient.shape
    pair_slots = clips_here // devices
    rows = clips_here * frames
    piece = frames // groups
    own = rows // groups
    clip_order = jnp.arange(clips_here, dtype=jnp.int32)
    target = clip_home // clips_here
    slot_place = clip_home % clips_here
    earlier = clip_order[None, :] < clip_order[:, None]
    same_target = target[None, :] == target[:, None]
    bucket_rank = jnp.sum((earlier & same_target).astype(jnp.int32), axis=1)
    bucket = target * pair_slots + bucket_rank
    in_bucket = (clip_order[:, None] == bucket[None, :]).astype(jnp.int32)

    def by_bucket(values):
        return jnp.sum(in_bucket * values[None, :], axis=1)

    first_row = by_bucket((clip_order // CPS) * sequence_rows + clip_offset)
    lengths = by_bucket(clip_length)
    places = by_bucket(slot_place)
    frame = jnp.arange(frames, dtype=jnp.int32).reshape(groups, 1, piece)
    source = jnp.where(
        frame < lengths[None, :, None], first_row[None, :, None] + frame, -1
    ).reshape(rows)
    goal = (places[:, None] * piece + jnp.arange(piece, dtype=jnp.int32)[None, :]).reshape(own)
    marks = (goal[:, None] == jnp.arange(own, dtype=jnp.int32)[None, :]).astype(BF)
    marks = marks.reshape(devices, pair_slots * piece, own)

    def by_part(values):
        return (
            values.reshape(clips_here, groups, piece, depth).swapaxes(0, 1).reshape(rows, depth)
        )

    part, width = up_weight.shape
    share = depth // groups
    vmem = pl.BlockSpec(memory_space=pltpu.VMEM)
    anywhere = pl.BlockSpec(memory_space=pl.ANY)
    exchange = (devices, own // devices, depth)
    input_parts, up_gradient, down_gradient = pl.pallas_call(
        fused_kernel,
        out_shape=(
            jax.ShapeDtypeStruct((groups, own, share), BF),
            jax.ShapeDtypeStruct((part, width), F32),
            jax.ShapeDtypeStruct((part, width), F32),
        ),
        in_specs=[anywhere, vmem, anywhere] + [vmem] * 6,
        out_specs=(vmem, vmem, vmem),
        scratch_shapes=[
            pltpu.VMEM((sequences * sequence_rows, columns), BF),
            pltpu.VMEM((depth, columns), BF),
            pltpu.VMEM((rows, columns), BF),
            pltpu.VMEM((2, devices, part, width), BF),
            pltpu.VMEM(marks.shape, BF),
            pltpu.VMEM((rows, depth), BF),
            pltpu.VMEM((3, own, depth), BF),
            pltpu.VMEM(exchange, BF),
            pltpu.VMEM(exchange, BF),
            pltpu.VMEM((rows, depth), BF),
            pltpu.VMEM((rows, depth), BF),
            pltpu.VMEM((depth, rows), BF),
            pltpu.VMEM((rows, depth), BF),
            pltpu.VMEM((depth, rows), BF),
            pltpu.VMEM((rows, width), BF),
            pltpu.VMEM((rows, width), F32),
            pltpu.VMEM((rows, width), BF),
            pltpu.VMEM((3, own, depth), BF),
            pltpu.VMEM((2, 4, part, width), F32),
            pltpu.VMEM((2, 4, part, width), BF),
            pltpu.VMEM((2, 4, part, width), BF),
            pltpu.VMEM((2, 4, part, width), BF),
            pltpu.VMEM((2, 5, part, width), BF),
            pltpu.VMEM((groups, own, share), BF),
            pltpu.SemaphoreType.DMA((2,)),
            pltpu.SemaphoreType.DMA((COPIES,)),
            pltpu.SemaphoreType.DMA((COPIES,)),
        ],
        compiler_params=pltpu.CompilerParams(
            collective_id=0, has_side_effects=True, vmem_limit_bytes=62 * 1024 * 1024
        ),
    )(
        token_gradient.reshape(sequences * sequence_rows, columns),
        source.reshape(rows, 1),
        projection,
        marks,
        by_part(block_input),
        by_part(block_output),
        jnp.stack([norm_gain, norm_bias, post_gain, up_bias]),
        up_weight,
        down_weight.T,
    )
    input_gradient = (
        input_parts.reshape(groups, clips_here, piece, share)
        .swapaxes(0, 1)
        .reshape(clips_here, frames, share)
    )
    return (input_gradient, up_gradient, down_gradient.T)


def solution(mesh):
    fused = mesh.shape["llm"] == 4 and mesh.shape["enc"] == 8
    return jax.shard_map(
        fused_shards if fused else shards,
        mesh=mesh,
        in_specs=(
            P("enc", None, "llm"),
            P(None, "llm"),
            P("enc"),
            P("enc"),
            P("enc"),
            P("enc", None, None),
            P("enc", None, None),
            P(),
            P(),
            P("enc", "llm"),
            P("llm"),
            P("llm", "enc"),
            P(),
        ),
        out_specs=(P("enc", None, "llm"), P("enc", "llm"), P("llm", "enc")),
        check_vma=False,
    )
```
